256 devices in a mesh: dp: 8 (over x, core), mp: 32 (over y, z).
Axes of the slice: x: 4, y: 4, z: 8, core: 2. Of those that a mesh axis runs over, the one named last changes fastest.
Arguments:
- x_in: bfloat16 [4096, 12288], P('dp', 'mp'), may hold values from -0.25 to 0.25
- grad_pre: bfloat16 [4096, 24576], P('dp', 'mp'), may hold values from -6 to 6
- weight_blocks: bfloat16 [4096, 128, 128], P('mp'), may hold values from -0.125 to 0.125
- slot_row: int32 [4096], P('mp'), may hold values from 0 to 2
- slot_col: int32 [4096], P('mp'), may hold values from 0 to 191, as said below
- slot_count: int32 [32], P('mp'), may hold values from 32 to 128, as said below
Outputs:
- grad_x: bfloat16 [4096, 12288], P('dp', 'mp')
- grad_blocks: float32 [4096, 128, 128], P('mp', 'dp')
The draws below stay inside these ranges and needn't reach their ends.
Inputs may be any that keep to these rules, and one draw needn't show every extreme that they name: `slot_col`: of each owner's 128 slots the first slot_count are live and name distinct (row, column) pairs; the rest hold indices in range and are ignored. The live slots of one owner name at most 2 distinct block-columns among the 6 block-columns c with c // 6 equal to any one index of mp, and one owner names exactly 2 of every such range. `slot_count`: some owner fills all of its slots.
All inputs are finite; a program needn't handle non-finite values.
Results may differ from the reference program's by a relative error of at most 0.001.
Values may be sent and summed in bfloat16 or wider, within the bound.
No kernel may reach another device: no remote copies, remote signals or barrier semaphores. Data moves between devices by JAX's collectives and lax.ppermute only.
A program may use at most 192 MiB of HBM per device.

```python
import jax
import jax.numpy as jnp
from jax import lax

D = 12288
H = 24576
BS = 128
CAP = 2
TOKENS = 4096
RB_DEV = 3
CB_DEV = 6
MAXB = 128
N_MP = 32


def pattern(key):
    keys = jax.random.split(key, 6)
    heavy = jax.random.randint(keys[0], (), 0, N_MP)
    owner = jnp.arange(N_MP)[:, None, None]
    kount = jax.random.randint(keys[1], (N_MP, N_MP, 1), 1, CAP + 1)
    kount = jnp.where(owner == heavy, CAP, kount)
    scores = jax.random.randint(keys[2], (N_MP, N_MP, CB_DEV), 0, 1 << 20) * CB_DEV + jnp.arange(CB_DEV)
    order = jnp.argsort(scores, axis=-1)[:, :, :CAP]
    first = jax.random.randint(keys[3], (N_MP, N_MP, CAP), 0, RB_DEV)
    offset = jax.random.randint(keys[4], (N_MP, N_MP, CAP), 1, RB_DEV)
    second = (first + offset) % RB_DEV
    extra = (jax.random.randint(keys[5], (N_MP, N_MP, CAP), 0, 4) == 0) | (owner == heavy)
    used = jnp.arange(CAP)[None, None, :] < kount
    source = jnp.arange(N_MP)[None, :, None]
    cols = source * CB_DEV + order
    live = jnp.stack([used, used & extra], -1).reshape(N_MP, MAXB).astype(jnp.int32)
    rows = jnp.stack([first, second], -1).reshape(N_MP, MAXB)
    colsx = jnp.stack([cols, cols], -1).reshape(N_MP, MAXB)
    rank_key = (1 - live) * MAXB + jnp.arange(MAXB)[None, :]
    perm = jnp.argsort(rank_key, axis=1)
    rows = jnp.take_along_axis(rows, perm, axis=1)
    colsx = jnp.take_along_axis(colsx, perm, axis=1)
    count = jnp.sum(live, axis=1)
    return (rows.reshape(-1).astype(jnp.int32), colsx.reshape(-1).astype(jnp.int32), count.astype(jnp.int32))


def draw_slot_row(key, part):
    return pattern(key)[0]


def draw_slot_col(key, part):
    return pattern(key)[1]


def draw_slot_count(key, part):
    return pattern(key)[2]


def levels(key, dims, pieces, low, high):
    level, own = 1.0, jax.random.fold_in(key, 6)
    for position, shards_of in pieces:
        steps = jnp.exp(jax.random.uniform(jax.random.fold_in(own, position), (shards_of,), jnp.float32, low / len(pieces), high / len(pieces)))
        level = level * jnp.repeat(steps, dims[position] // shards_of).reshape([-1 if axis == position else 1 for axis in range(len(dims))])
    return level


def gaussian(stream_key, dims, scale, reach, shards=(), held_as=jnp.bfloat16):
    entries = scale * jax.random.normal(stream_key, dims, jnp.float32)
    if shards:
        entries = entries * levels(stream_key, dims, shards, -0.22, 0.18)
    return jnp.clip(entries, -reach, reach).astype(held_as)


def setup_inputs(seed: int = 0) -> dict:
    key_list = jax.random.split(jax.random.key(seed), 7)
    x_in = gaussian(key_list[0], (TOKENS, D), (TOKENS ** -0.5), 0.25, ((0, 8), (1, 32)))
    grad_pre = gaussian(key_list[1], (TOKENS, H), 1.0, 6.0, ((0, 8), (1, 32)))
    weight_blocks = gaussian(key_list[2], (N_MP * MAXB, BS, BS), (16 * BS) ** -0.5, 0.125, ((0, 32),))
    slot_row = draw_slot_row(jax.random.fold_in(key_list[6], 71), 0)
    slot_col = draw_slot_col(jax.random.fold_in(key_list[6], 71), 0)
    slot_count = draw_slot_count(jax.random.fold_in(key_list[6], 71), 0)
    return dict(x_in=x_in, grad_pre=grad_pre, weight_blocks=weight_blocks, slot_row=slot_row, slot_col=slot_col, slot_count=slot_count)


def reference(x_in, grad_pre, weight_blocks, slot_row, slot_col, slot_count):
    high = lax.Precision.HIGHEST
    x_three = x_in.reshape(TOKENS, D // BS, BS)
    p_three = grad_pre.reshape(TOKENS, H // BS, BS)

    def owner(index):
        start = (index * MAXB).astype(jnp.int32)
        rows = lax.dynamic_slice_in_dim(slot_row, start, MAXB, 0)
        cols = lax.dynamic_slice_in_dim(slot_col, start, MAXB, 0)
        weights = lax.dynamic_slice_in_dim(weight_blocks, start, MAXB, 0).astype(jnp.float32)
        alive = (jnp.arange(MAXB) < slot_count[index]).astype(jnp.float32)
        global_rows = (index * RB_DEV + rows).astype(jnp.int32)
        x_blocks = jnp.take(x_three, global_rows, axis=1).astype(jnp.float32)
        p_blocks = jnp.take(p_three, cols, axis=1).astype(jnp.float32)
        grads = jnp.einsum("tgj,tgk->gjk", x_blocks, p_blocks, precision=high) * alive[:, None, None]
        contrib = jnp.einsum("tgk,gjk->tgj", p_blocks, weights, precision=high)
        place = (rows[:, None] == jnp.arange(RB_DEV)[None, :]).astype(jnp.float32) * alive[:, None]
        part = jnp.einsum("tgj,gr->trj", contrib, place, precision=high)
        return part, grads

    parts, grads = lax.map(owner, jnp.arange(N_MP))
    grad_x = jnp.transpose(parts, (1, 0, 2, 3)).reshape(TOKENS, D).astype(jnp.bfloat16)
    return grad_x, grads.reshape(N_MP * MAXB, BS, BS)
```

```python
import jax
import jax.numpy as jnp
from jax import lax
from jax.experimental import pallas as pl
from jax.experimental.pallas import tpu as pltpu
from jax.sharding import PartitionSpec as P

NY, NZ = 4, 8
NX = 4
B = 128
T = 512
CB, RB = 6, 3
SLOTS = 128
GROUPS = ((0,), (1, -1), (2, -2), (3, -3), (4,))
SENDS = (1, -1, 2)
SOURCE_DY = (0, -1, 1, -2)
DY_PART = (0, 2, 3, 1)

VMEM = pl.BlockSpec(memory_space=pltpu.VMEM)
SMEM = pl.BlockSpec(memory_space=pltpu.SMEM)
PARAMS = pltpu.CompilerParams(vmem_limit_bytes=48 << 20)
F32, BF16, I32 = jnp.float32, jnp.bfloat16, jnp.int32


def sds(shape, dtype):
    return jax.ShapeDtypeStruct(shape, dtype)


def cost(flops, moved):
    return pl.CostEstimate(flops=flops, bytes_accessed=moved, transcendentals=0)


def source_of(me, dy, dz):
    y, z = me >> 3, me & 7
    return (((y + dy) & (NY - 1)) << 3) + ((z + dz) & (NZ - 1))


def tables_kernel(row, col, count, need, inv, pos):
    n = NY * NZ

    @pl.loop(0, n)
    def _(i):
        need[i] = CB
        need[n + i] = -1

    @pl.loop(0, n * 2 * RB)
    def _(i):
        inv[i] = -1

    @pl.loop(0, count[0])
    def _(s):
        src = col[s] // CB
        c = col[s] - src * CB
        need[src] = jnp.minimum(need[src], c)
        need[n + src] = jnp.maximum(need[n + src], c)

    @pl.loop(0, n)
    def _(i):
        none = need[n + i] < 0
        need[i] = jnp.where(none, 0, need[i])
        need[n + i] = jnp.where(none, 0, need[n + i])

    @pl.loop(0, SLOTS)
    def _(s):
        src = col[s] // CB
        c = col[s] - src * CB
        at = src * (2 * RB) + jnp.where(c == need[src], 0, RB) + row[s]
        live = s < count[0]
        pos[s] = jnp.where(live, at, -1)

        @pl.when(live)
        def _():
            inv[at] = s


def tables(slot_row, slot_col, slot_count):
    return pl.pallas_call(
        tables_kernel,
        out_shape=(sds((2 * NY * NZ,), I32), sds((NY * NZ * 2 * RB,), I32), sds((SLOTS,), I32)),
        in_specs=[SMEM] * 3,
        out_specs=(SMEM,) * 3,
        name="tables",
    )(slot_row, slot_col, slot_count)


def dense_kernel(me, inv, w, *outs):
    for group, out in zip(GROUPS, outs):
        for part, dy in enumerate(SOURCE_DY):
            for at, dz in enumerate(group):
                src = source_of(me[0], dy, dz)

                @pl.loop(0, 2)
                def _(p):
                    for r in range(RB):
                        s = inv[src * (2 * RB) + p * RB + r]
                        blk = w[jnp.maximum(s, 0)]
                        blk = jnp.where(s >= 0, blk, jnp.zeros_like(blk))
                        lanes = pl.ds(pl.multiple_of((2 * at + p) * B, B), B)
                        out[part, r * B : (r + 1) * B, lanes] = blk


def dense(me, inv, w):
    return pl.pallas_call(
        dense_kernel,
        out_shape=tuple(sds((4, RB * B, 2 * B * len(g)), BF16) for g in GROUPS),
        in_specs=[SMEM, SMEM, VMEM],
        out_specs=(VMEM,) * len(GROUPS),
        compiler_params=PARAMS,
        cost_estimate=cost(0, 20 << 20),
        name="dense",
    )(me, inv, w)


def turn_kernel(d, x, out, held):
    held[...] = x[...].T
    dx, dc = d[0] >> 1, d[0] & 1
    for cc in range(2):
        for xx in range(NX):
            to = (((dx + xx) & (NX - 1)) << 1) + (dc ^ cc)
            for r in range(RB):
                rows = pl.ds(pl.multiple_of(r * B + to * 16, 16), 16)
                at = ((cc * NX + xx) * RB + r) * 16
                out[at : at + 16, :] = held[rows, :]


def turn(d, x):
    return pl.pallas_call(
        turn_kernel,
        out_shape=sds((RB * B, T), BF16),
        in_specs=[SMEM, VMEM],
        out_specs=VMEM,
        scratch_shapes=[pltpu.VMEM((RB * B, T), BF16)],
        compiler_params=PARAMS,
        cost_estimate=cost(0, 1 << 20),
        name="turn",
    )(d, x)


def select_kernel(group, me, n0, n1, n2, n3, *refs):
    gs, outs = refs[: len(group)], refs[len(group) :]
    for at, dz in enumerate(group):
        src = source_of(me[0], 0, dz)
        for need, out in zip((n0, n1, n2, n3), outs):
            for p in range(2):
                c = need[p * NY * NZ + src]
                lanes = pl.ds(pl.multiple_of(c * B, B), B)
                out[:, (2 * at + p) * B : (2 * at + p + 1) * B] = gs[at][:, lanes]


def select(group, me, needs, gs):
    n = len(group)
    return pl.pallas_call(
        lambda *refs: select_kernel(group, *refs),
        out_shape=tuple(sds((T, 2 * B * n), BF16) for _ in range(4)),
        in_specs=[SMEM] * 5 + [VMEM] * n,
        out_specs=(VMEM,) * 4,
        compiler_params=PARAMS,
        cost_estimate=cost(0, n << 21),
        name="select",
    )(me, *needs, *gs)


def products_kernel(first, last, *refs):
    xt, b0, b1, b2, b3, w = refs[:6]
    rest = refs[6:]
    acc = None
    if not first:
        acc, rest = rest[0][...], rest[1:]
    total, mine, other = rest
    width = b0.shape[1]
    half = RB * B // 2
    for part, b in enumerate((b0, b1, b2, b3)):
        blk = b[...]
        prod = lax.dot_general(blk, w[part], (((1,), (1,)), ((), ())), preferred_element_type=F32)
        acc = prod if acc is None else acc + prod
        grads = jnp.dot(xt[...], blk, preferred_element_type=F32)
        mine[:, part * width : (part + 1) * width] = grads[:half]
        other[:, part * width : (part + 1) * width] = grads[half:]
    total[...] = acc.astype(total.dtype)


def products(first, last, xt, blocks, w, acc):
    width = blocks[0].shape[1]
    half = RB * B // 2
    args = (xt, *blocks, w) + (() if first else (acc,))
    flops = 2 * 2 * 4 * width * T * RB * B
    moved = 4 * T * width * 2 + 4 * RB * B * width * 6 + 8 * T * RB * B
    return pl.pallas_call(
        lambda *refs: products_kernel(first, last, *refs),
        out_shape=(
            sds((T, RB * B), BF16 if last else F32),
            sds((half, 4 * width), F32),
            sds((half, 4 * width), F32),
        ),
        in_specs=[VMEM] * len(args),
        out_specs=(VMEM,) * 3,
        compiler_params=PARAMS,
        cost_estimate=cost(flops, moved),
        name="products",
    )(*args)


def pair_kernel(mine, theirs, *outs):
    step = RB * 16
    for i, out in enumerate(outs):
        rows = slice(i * step, (i + 1) * step)
        out[...] = mine[rows, :] + theirs[rows, :]


def pair(mine, theirs):
    width = mine.shape[1]
    return pl.pallas_call(
        pair_kernel,
        out_shape=tuple(sds((RB * 16, width), F32) for _ in range(NX)),
        in_specs=[VMEM] * 2,
        out_specs=(VMEM,) * NX,
        compiler_params=PARAMS,
        cost_estimate=cost(0, 3 * mine.shape[0] * width * 4),
        name="pair",
    )(mine, theirs)


def slots_kernel(me, pos, *refs):
    ins, out, held = refs[:-2], refs[-2], refs[-1]
    wide = 2 * B
    for i, group in enumerate(GROUPS):
        a, b, c, d = (ref[...] for ref in ins[4 * i : 4 * i + 4])
        total = (a + b) + (c + d)
        for part in range(4):
            for at, dz in enumerate(group):
                lo = (part * len(group) + at) * wide
                held[dz & (NZ - 1), part] = total[:, lo : lo + wide]
    y, z = me[0] >> 3, me[0] & 7

    @pl.loop(0, SLOTS)
    def _(s):
        at = pos[s]
        safe = jnp.maximum(at, 0)
        src = safe // (2 * RB)
        rest = safe - src * (2 * RB)
        p = jnp.where(rest >= RB, 1, 0)
        r = rest - RB * p
        dz = ((src & 7) - z) & (NZ - 1)
        dy = ((src >> 3) - y) & (NY - 1)
        part = jnp.where(dy == 0, 0, jnp.where(dy == 1, DY_PART[1], jnp.where(dy == 2, DY_PART[2], DY_PART[3])))
        rows = pl.ds(pl.multiple_of(r * 16, 16), 16)
        lanes = pl.ds(pl.multiple_of(p * B, B), B)
        blk = held[dz, part, rows, lanes]
        out[s] = jnp.where(at >= 0, blk, jnp.zeros_like(blk))


def slots(me, pos, parts):
    return pl.pallas_call(
        slots_kernel,
        out_shape=sds((SLOTS, 16, B), F32),
        in_specs=[SMEM, SMEM] + [VMEM] * len(parts),
        out_specs=VMEM,
        scratch_shapes=[pltpu.VMEM((NZ, 4, RB * 16, 2 * B), F32)],
        compiler_params=PARAMS,
        cost_estimate=cost(0, 9 << 20),
        name="slots",
    )(me, pos, *parts)


def shift_z(k):
    return [(y * NZ + z, y * NZ + (z + k) % NZ) for y in range(NY) for z in range(NZ)]


def shift_y(k):
    return [(y * NZ + z, (y + k) % NY * NZ + z) for y in range(NY) for z in range(NZ)]


def shift_x(k):
    return [(x * 2 + c, (x + k) % NX * 2 + c) for x in range(NX) for c in range(2)]


def on_device(x_in, grad_pre, weight_blocks, slot_row, slot_col, slot_count):
    me = lax.axis_index("mp").astype(I32).reshape(1)
    d = lax.axis_index("dp").astype(I32).reshape(1)
    held = {0: grad_pre}
    for k in range(1, NZ // 2 + 1):
        held[-k] = lax.ppermute(held[1 - k], "mp", shift_z(1))
        if k < NZ // 2:
            held[k] = lax.ppermute(held[k - 1], "mp", shift_z(-1))
    held[4] = held[-4]
    need, inv, pos = tables(slot_row, slot_col, slot_count)
    needs = [need] + [lax.ppermute(need, "mp", shift_y(-k)) for k in SENDS]
    xt = turn(d, x_in)
    weights = dense(me, inv, weight_blocks)
    acc, parts = None, []
    for i, group in enumerate(GROUPS):
        own, *sent = select(group, me, needs, [held[dz] for dz in group])
        blocks = [own] + [lax.ppermute(a, "mp", shift_y(k)) for a, k in zip(sent, SENDS)]
        acc, mine, other = products(i == 0, i == len(GROUPS) - 1, xt, blocks, weights[i], acc)
        theirs = lax.ppermute(other, "dp", [(a, a ^ 1) for a in range(2 * NX)])
        keep, *out = pair(mine, theirs)
        parts += [keep] + [lax.ppermute(a, "dp", shift_x(k)) for a, k in zip(out, (1, 2, 3))]
    return acc, slots(me, pos, parts)


def solution(mesh):
    placed = (P("dp", "mp"), P("dp", "mp"), P("mp", None, None), P("mp"), P("mp"), P("mp"))
    return jax.shard_map(
        on_device,
        mesh=mesh,
        in_specs=placed,
        out_specs=(P("dp", "mp"), P("mp", "dp", None)),
        check_vma=False,
    )
```

```python
import jax
import jax.numpy as jnp
from jax import lax
from jax.experimental import pallas as pl
from jax.experimental.pallas import tpu as pltpu
from jax.sharding import PartitionSpec as P

NY, NZ = 4, 8
NX = 4
B = 128
T = 512
CB, RB = 6, 3
D = RB * B
SLOTS = 128
EARLY, LATE = (0, 1, -1, 2, -2), (3, -3, 4)
ORDER = EARLY + LATE
ROUNDS = ((0, 1, -1, 2, -2, 3, -3), (4,))
OWNERS = (1, -1, 2)
DY_PART = (0, 2, 3, 1)
HEAD = 16

VMEM = pl.BlockSpec(memory_space=pltpu.VMEM)
SMEM = pl.BlockSpec(memory_space=pltpu.SMEM)
PARAMS = pltpu.CompilerParams(vmem_limit_bytes=48 << 20)
F32, BF16, I32 = jnp.float32, jnp.bfloat16, jnp.int32


def sds(shape, dtype):
    return jax.ShapeDtypeStruct(shape, dtype)


def cost(flops, moved):
    return pl.CostEstimate(flops=flops, bytes_accessed=moved, transcendentals=0)


def source_column(col):
    src = (col * 43691) >> 18
    return src, col - src * CB


def need_kernel(col, count, need):
    shape = (NY * NZ, SLOTS)
    src, c = source_column(col[...])
    slot = lax.broadcasted_iota(I32, shape, 1)
    hit = (src == lax.broadcasted_iota(I32, shape, 0)) & (slot < count[0])
    lo = jnp.min(jnp.where(hit, c, CB), axis=1, keepdims=True)
    hi = jnp.max(jnp.where(hit, c, -1), axis=1, keepdims=True)
    none = hi < 0
    need[...] = jnp.where(slot == 0, jnp.where(none, 0, lo), jnp.where(none, 0, hi))


def need_table(slot_col, slot_count):
    return pl.pallas_call(
        need_kernel,
        out_shape=sds((NY * NZ, SLOTS), I32),
        in_specs=[VMEM, SMEM],
        out_specs=VMEM,
        cost_estimate=cost(0, 1 << 14),
        name="need",
    )(slot_col.reshape(1, SLOTS), slot_count)


def pack_kernel(me, d, row, col, count, need, w, own, b1, b2, b3, held):
    y = me[0] >> 3
    held[...] = jnp.zeros_like(held)

    @pl.loop(0, SLOTS, unroll=4)
    def _(s):
        src, c = source_column(col[s])
        p = jnp.where(c == need[src, 0], 0, 1)
        at = jnp.where(s < count[0], (src - (y << 3)) & (NY * NZ - 1), NY * NZ)
        rows = pl.ds(pl.multiple_of(row[s] * B, B), B)
        held[at, rows, pl.ds(pl.multiple_of(p * B, B), B)] = w[s]

    own[...] = held[:NZ]
    lo = (d[0] & 1) * (NZ // 2)
    for out, t in ((b1, 3), (b2, 1), (b3, 2)):
        out[...] = held[pl.ds(t * NZ + lo, NZ // 2)]


def pack(me, d, slot_row, slot_col, slot_count, need, w):
    part = sds((NZ // 2, D, 2 * B), BF16)
    return pl.pallas_call(
        pack_kernel,
        out_shape=(sds((NZ, D, 2 * B), BF16), part, part, part),
        in_specs=[SMEM] * 6 + [VMEM],
        out_specs=(VMEM,) * 4,
        scratch_shapes=[pltpu.VMEM((NY * NZ + 1, D, 2 * B), BF16)],
        compiler_params=PARAMS,
        cost_estimate=cost(0, 7 << 20),
        name="pack",
    )(me, d, slot_row, slot_col, slot_count, need, w)


def two_columns(g, cols, part, src, sel):
    for p in range(2):
        lanes = pl.ds(pl.multiple_of(cols[part, p * NY * NZ + src] * B, B), B)
        sel[:, p * B : (p + 1) * B] = g[:, lanes]
    return sel[...]


def early_kernel(me, cols, *refs):
    xts, gs, (out, sel) = refs[:4], refs[4:-2], refs[-2:]
    lo = 0
    for part in range(4):
        for i, dz in enumerate(EARLY):
            src = (me[0] & ~(NZ - 1)) + ((me[0] + dz) & (NZ - 1))
            blk = two_columns(gs[i], cols, part, src, sel.at[(part * len(EARLY) + i) % 2])
            out[:, lo : lo + 2 * B] = jnp.dot(xts[part][HEAD:, :], blk, preferred_element_type=F32)
            lo += 2 * B


def early(me, cols, xts, gs):
    width = 4 * 2 * B * len(gs)
    return pl.pallas_call(
        early_kernel,
        out_shape=sds((D, width), F32),
        in_specs=[SMEM] * 2 + [VMEM] * (4 + len(gs)),
        out_specs=VMEM,
        scratch_shapes=[pltpu.VMEM((2, T, 2 * B), BF16)],
        compiler_params=PARAMS,
        cost_estimate=cost(2 * width * T * D, D * width * 4 + len(gs) * T * CB * B * 2 + 8 * T * D),
        name="early",
    )(me, cols, *xts, *gs)


def late_kernel(me, d, cols, *refs):
    xts, gs, (mine, other, turned, sel) = refs[:4], refs[4:-4], refs[-4:]
    half, step = D // 2, RB * 16
    dx, dc = d[0] >> 1, d[0] & 1
    lo = 0
    for part in range(4):
        for cc in range(2):
            for xx in range(NX):
                to = (((dx + xx) & (NX - 1)) << 1) + (dc ^ cc)
                rows = pl.ds(pl.multiple_of(HEAD + to * step, 16), step)
                at = (cc * NX + xx) * step
                turned[at : at + step, :] = xts[part][rows, :]
        for i, dz in enumerate(LATE):
            src = (me[0] & ~(NZ - 1)) + ((me[0] + dz) & (NZ - 1))
            blk = two_columns(gs[i], cols, part, src, sel.at[(part * len(LATE) + i) % 2])
            prod = jnp.dot(turned[...], blk, preferred_element_type=F32)
            mine[:, lo : lo + 2 * B] = prod[:half]
            other[:, lo : lo + 2 * B] = prod[half:]
            lo += 2 * B
    for out in (mine, other):
        out[:, lo:] = jnp.zeros((half, B), F32)


def late(me, d, cols, xts, gs):
    width = 4 * 2 * B * len(gs)
    return pl.pallas_call(
        late_kernel,
        out_shape=(sds((D // 2, width + B), F32),) * 2,
        in_specs=[SMEM] * 3 + [VMEM] * (4 + len(gs)),
        out_specs=(VMEM,) * 2,
        scratch_shapes=[pltpu.VMEM((D, T), BF16), pltpu.VMEM((2, T, 2 * B), BF16)],
        compiler_params=PARAMS,
        cost_estimate=cost(2 * width * T * D, D * width * 4 + len(gs) * T * CB * B * 2 + 8 * T * D),
        name="late",
    )(me, d, cols, *xts, *gs)


def inputs_kernel(stage, first, me, d, cols, own, near, far, *refs):
    gs, refs = refs[: len(stage)], refs[len(stage) :]
    accs, outs, sel = refs[:-5], refs[-5:-1], refs[-1]
    for part in (1, 2, 3, 0):
        total = None if first else accs[part][...]
        for i, dz in enumerate(stage):
            z = (me[0] + dz) & (NZ - 1)
            src = (me[0] & ~(NZ - 1)) + z
            blk = two_columns(gs[i], cols, part, src, sel.at[i % 2])
            if part == 0:
                w = own[z]
            else:
                at = z & (NZ // 2 - 1)
                mine = (z >> 2) == (d[0] & 1)
                w = jnp.where(mine, near[part - 1, at], far[part - 1, at])
            prod = lax.dot_general(blk, w, (((1,), (1,)), ((), ())), preferred_element_type=F32)
            total = prod if total is None else total + prod
        outs[part][...] = total


def inputs(stage, me, d, cols, own, near, far, gs, accs):
    first = not accs
    flops = 4 * 2 * T * D * 2 * B * len(stage)
    return pl.pallas_call(
        lambda *refs: inputs_kernel(stage, first, *refs),
        out_shape=(sds((T, D), F32),) * 4,
        in_specs=[SMEM] * 3 + [VMEM] * (3 + len(gs) + len(accs)),
        out_specs=(VMEM,) * 4,
        scratch_shapes=[pltpu.VMEM((2, T, 2 * B), BF16)],
        compiler_params=PARAMS,
        cost_estimate=cost(flops, 10 << 20),
        name="inputs",
    )(me, d, cols, own, near, far, *gs, *accs)


def turn_kernel(need, x, out):
    n = NY * NZ
    lane = lax.broadcasted_iota(I32, (HEAD, T), 1)
    head = jnp.zeros((HEAD, T), I32)
    for i in range(n):
        head = jnp.where(lane == i, need[i, 0], head)
        head = jnp.where(lane == n + i, need[i, 1], head)
    out[:HEAD, :] = head.astype(F32).astype(BF16)
    held = x[...].T
    for to in range(2 * NX):
        for r in range(RB):
            at = HEAD + (to * RB + r) * 16
            out[at : at + 16, :] = held[r * B + to * 16 : r * B + to * 16 + 16, :]


def turn(need, x):
    return pl.pallas_call(
        turn_kernel,
        out_shape=sds((HEAD + D, T), BF16),
        in_specs=[SMEM, VMEM],
        out_specs=VMEM,
        compiler_params=PARAMS,
        cost_estimate=cost(0, 1 << 20),
        name="turn",
    )(need, x)


def slots_kernel(me, row, col, count, need, *refs):
    ins, out, held = refs[:-2], refs[-2], refs[-1]
    wide = 2 * B
    for part in range(4):
        for i, dz in enumerate(ORDER):
            held[dz & (NZ - 1), part] = ins[part][:, i * wide : (i + 1) * wide]
    y, z = me[0] >> 3, me[0] & 7

    @pl.loop(0, SLOTS, unroll=4)
    def _(s):
        src, c = source_column(col[s])
        p = jnp.where(c == need[src, 0], 0, 1)
        dz = ((src & 7) - z) & (NZ - 1)
        dy = ((src >> 3) - y) & (NY - 1)
        part = jnp.where(dy == 0, DY_PART[0], jnp.where(dy == 1, DY_PART[1], jnp.where(dy == 2, DY_PART[2], DY_PART[3])))
        rows = pl.ds(pl.multiple_of(row[s] * 16, 16), 16)
        lanes = pl.ds(pl.multiple_of(p * B, B), B)
        blk = held[dz, part, rows, lanes]
        out[s] = jnp.where(s < count[0], blk, jnp.zeros_like(blk))


def slots(me, row, col, count, need, parts):
    return pl.pallas_call(
        slots_kernel,
        out_shape=sds((SLOTS, 16, B), F32),
        in_specs=[SMEM] * 5 + [VMEM] * len(parts),
        out_specs=VMEM,
        scratch_shapes=[pltpu.VMEM((NZ, 4, RB * 16, 2 * B), F32)],
        compiler_params=PARAMS,
        cost_estimate=cost(0, 5 << 20),
        name="slots",
    )(me, row, col, count, need, *parts)


def shift_z(k):
    return [(y * NZ + z, y * NZ + (z + k) % NZ) for y in range(NY) for z in range(NZ)]


def shift_y(k):
    return [(y * NZ + z, (y + k) % NY * NZ + z) for y in range(NY) for z in range(NZ)]


def shift_x(k):
    return [(x * 2 + c, (x + k) % NX * 2 + c) for x in range(NX) for c in range(2)]


def tie(*trees):
    return lax.optimization_barrier(trees)


def after(a, first):
    return lax.optimization_barrier((a, first))[0]


def tie(*trees):
    return lax.optimization_barrier(trees)


def on_device(x_in, grad_pre, weight_blocks, slot_row, slot_col, slot_count):
    me = lax.axis_index("mp").astype(I32).reshape(1)
    d = lax.axis_index("dp").astype(I32).reshape(1)
    step = RB * 16

    def z_step(a, k):
        return lax.ppermute(a, "mp", shift_z(k))

    def core_step(a):
        return lax.ppermute(a, "dp", [(a, a ^ 1) for a in range(2 * NX)])

    def y_back(parts):
        return [lax.ppermute(a, "mp", shift_y(k)) for a, k in zip(parts, OWNERS)]

    def pair_step(mine, theirs):
        rows = [mine[i * step : (i + 1) * step] + theirs[i * step : (i + 1) * step] for i in range(NX)]
        top = jnp.max(jnp.abs(mine[step:] + theirs[step:]))
        power = jnp.floor(jnp.log2(2.0**14 / jnp.maximum(top, 1e-30)))
        scale = jnp.exp2(power)
        inside = lax.broadcasted_iota(I32, rows[0].shape, 1) < rows[0].shape[1] - B
        return rows[0], [jnp.where(inside, a * scale, power).astype(jnp.float16) for a in rows[1:]]

    def x_step(out):
        return [lax.ppermute(a, "dp", shift_x(k)) for a, k in zip(out, (1, 2, 3))]

    def join(keep, got):
        a, b, c = (g.astype(F32) * jnp.exp2(-g[0, -1].astype(F32)) for g in got)
        return (keep + a) + (b + c)

    def by_part(sums):
        n = [2 * B * len(EARLY), 2 * B * len(LATE)]
        return [jnp.concatenate([a[:, p * k : (p + 1) * k] for a, k in zip(sums, n)], axis=1) for p in range(4)]

    held = {0: grad_pre}
    z1 = [z_step(grad_pre, 1), z_step(grad_pre, -1)]
    need = need_table(slot_col, slot_count)
    xt = turn(need, x_in)
    xts = [lax.ppermute(xt, "mp", shift_y(-k)) for k in OWNERS]
    own, *bufs = pack(me, d, slot_row, slot_col, slot_count, need, weight_blocks)
    z1, xts, bufs = tie(z1, xts, bufs)

    held[-1], held[1] = z1
    z2 = [z_step(z1[0], 1), z_step(z1[1], -1)]
    bufs = [lax.ppermute(a, "mp", shift_y(-k)) for a, k in zip(bufs, OWNERS)]
    xts = [xt, *xts]
    cols = jnp.stack([a[0, : 2 * NY * NZ] for a in xts]).astype(I32)
    z2, cols = tie(z2, cols)

    held[-2], held[2] = z2
    z3 = [z_step(z2[0], 1), z_step(z2[1], -1)]
    grads = early(me, cols, xts, [held[k] for k in EARLY])
    z3, bufs, grads = tie(z3, bufs, grads)
    early_sum = lax.psum_scatter(grads, "dp", scatter_dimension=0, tiled=True)

    held[-3], held[3] = z3
    half = T // 2
    z4 = [z_step(z3[0][:half], 1), z_step(z3[1][half:], -1)]
    near = jnp.stack(bufs)
    far = core_step(near)
    accs = inputs(ROUNDS[0], me, d, cols, own, near, far, [held[k] for k in ROUNDS[0]], ())
    z4, accs = tie(z4, accs)

    held[4] = jnp.concatenate(z4, axis=0)
    mine, other = late(me, d, cols, xts, [held[k] for k in LATE])
    theirs = core_step(other)
    accs = inputs(ROUNDS[1], me, d, cols, own, near, far, [after(held[4], other)], accs)
    totals = [accs[0], *y_back(accs[1:3])]
    keep, out = pair_step(mine, theirs)
    got = x_step(out)
    totals.append(lax.ppermute(after(accs[3], got), "mp", shift_y(OWNERS[2])))
    first, *back = by_part([early_sum, join(keep, got)])
    parts = [first, *y_back(back)]
    grad_x = ((totals[0] + totals[1]) + (totals[2] + totals[3])).astype(BF16)
    return grad_x, slots(me, slot_row, slot_col, slot_count, after(need, grad_x), parts)


def solution(mesh):
    placed = (P("dp", "mp"), P("dp", "mp"), P("mp", None, None), P("mp"), P("mp"), P("mp"))
    return jax.shard_map(
        on_device,
        mesh=mesh,
        in_specs=placed,
        out_specs=(P("dp", "mp"), P("mp", "dp", None)),
        check_vma=False,
    )
```

```python
import math

import jax
import jax.numpy as jnp
from jax import lax
from jax.experimental import pallas as pl
from jax.experimental.pallas import tpu as pltpu
from jax.sharding import PartitionSpec as P

NY, NZ = 4, 8
NX = 4
B = 128
T = 512
CB, RB = 6, 3
D = RB * B
SLOTS = 128
EARLY, LATE = (0, 1, -1, 2, -2), (3, -3, 4)
ORDER = EARLY + LATE
ROUNDS = ((0, 1, -1, 2, -2, 3, -3), (4,))
OWNERS = (1, -1, 2)
DY_PART = (0, 2, 3, 1)
HEAD = 16

VMEM = pl.BlockSpec(memory_space=pltpu.VMEM)
SMEM = pl.BlockSpec(memory_space=pltpu.SMEM)
PARAMS = pltpu.CompilerParams(vmem_limit_bytes=48 << 20)
F32, BF16, I32 = jnp.float32, jnp.bfloat16, jnp.int32


def sds(shape, dtype):
    return jax.ShapeDtypeStruct(shape, dtype)


def cost(flops, moved):
    return pl.CostEstimate(flops=flops, bytes_accessed=moved, transcendentals=0)


def source_column(col):
    src = (col * 43691) >> 18
    return src, col - src * CB


def turn_kernel(col, count, x, need, out):
    n = NY * NZ
    shape = (SLOTS, SLOTS)
    src, c = source_column(jnp.broadcast_to(col[...], shape).T)
    lane = lax.broadcasted_iota(I32, shape, 1)
    hit = (src == (lane & (n - 1))) & (lax.broadcasted_iota(I32, shape, 0) < count[0])
    lo = jnp.min(jnp.where(hit, c, CB), axis=0, keepdims=True)
    hi = jnp.max(jnp.where(hit, c, -1), axis=0, keepdims=True)
    row = jnp.where(hi < 0, 0, jnp.where(lane[:1] < n, lo, hi))
    need[...] = jnp.broadcast_to(row, need.shape)
    out[:HEAD, :] = jnp.zeros((HEAD, T), BF16)
    out[:HEAD, :SLOTS] = jnp.broadcast_to(row, (HEAD, SLOTS)).astype(F32).astype(BF16)
    held = x[...].T
    for to in range(2 * NX):
        for r in range(RB):
            at = HEAD + (to * RB + r) * 16
            out[at : at + 16, :] = held[r * B + to * 16 : r * B + to * 16 + 16, :]


def turn(slot_col, slot_count, x):
    return pl.pallas_call(
        turn_kernel,
        out_shape=(sds((8, SLOTS), I32), sds((HEAD + D, T), BF16)),
        in_specs=[VMEM, SMEM, VMEM],
        out_specs=(VMEM, VMEM),
        compiler_params=PARAMS,
        cost_estimate=cost(0, 1 << 20),
        name="turn",
    )(slot_col.reshape(1, SLOTS), slot_count, x)


def heads_kernel(a, b, c, d, out):
    for i, head in enumerate((a, b, c, d)):
        out[i : i + 1, :] = head[...].astype(F32).astype(I32)[:1]


def heads(xts):
    return pl.pallas_call(
        heads_kernel,
        out_shape=sds((4, SLOTS), I32),
        grid=(1,),
        in_specs=[pl.BlockSpec((HEAD, SLOTS), lambda i: (0, 0))] * 4,
        out_specs=pl.BlockSpec((4, SLOTS), lambda i: (0, 0)),
        cost_estimate=cost(0, 1 << 14),
        name="heads",
    )(*xts)


def pack_kernel(me, d, row, col, count, need, w, own, b1, b2, b3, held):
    y = me[0] >> 3
    held[...] = jnp.zeros_like(held)

    @pl.loop(0, SLOTS, unroll=4)
    def _(s):
        src, c = source_column(col[s])
        p = jnp.where(c == need[0, src], 0, 1)
        at = jnp.where(s < count[0], (src - (y << 3)) & (NY * NZ - 1), NY * NZ)
        rows = pl.ds(pl.multiple_of(p * B, B), B)
        held[at, rows, pl.ds(pl.multiple_of(row[s] * B, B), B)] = w[s].T

    own[...] = held[:NZ]
    lo = (d[0] & 1) * (NZ // 2)
    for out, t in ((b1, 3), (b2, 1), (b3, 2)):
        out[...] = held[pl.ds(t * NZ + lo, NZ // 2)]


def pack(me, d, slot_row, slot_col, slot_count, need, w):
    part = sds((NZ // 2, 2 * B, D), BF16)
    return pl.pallas_call(
        pack_kernel,
        out_shape=(sds((NZ, 2 * B, D), BF16), part, part, part),
        in_specs=[SMEM] * 6 + [VMEM],
        out_specs=(VMEM,) * 4,
        scratch_shapes=[pltpu.VMEM((NY * NZ + 1, 2 * B, D), BF16)],
        compiler_params=PARAMS,
        cost_estimate=cost(0, 7 << 20),
        name="pack",
    )(me, d, slot_row, slot_col, slot_count, need, w)


def two_columns(gs, cols, part, src, sel):
    for p in range(2):
        lanes = pl.ds(pl.multiple_of(cols[part, p * NY * NZ + src] * B, B), B)
        at = 0
        for g in gs:
            sel[at : at + g.shape[0], p * B : (p + 1) * B] = g[:, lanes]
            at += g.shape[0]
    return sel[...]


def by_source(stage, refs):
    refs = list(refs)
    return [[refs.pop(0) for _ in range(2 if dz == 4 else 1)] for dz in stage]


def early_kernel(me, cols, *refs):
    xts, gs, (out, sel) = refs[:4], by_source(EARLY, refs[4:-2]), refs[-2:]
    lo = 0
    for part in range(4):
        for i, dz in enumerate(EARLY):
            src = (me[0] & ~(NZ - 1)) + ((me[0] + dz) & (NZ - 1))
            blk = two_columns(gs[i], cols, part, src, sel.at[(part * len(EARLY) + i) % 2])
            out[:, lo : lo + 2 * B] = jnp.dot(xts[part][HEAD:, :], blk, preferred_element_type=F32)
            lo += 2 * B


def early(me, cols, xts, gs):
    width = 4 * 2 * B * len(gs)
    return pl.pallas_call(
        early_kernel,
        out_shape=sds((D, width), F32),
        in_specs=[SMEM] * 2 + [VMEM] * (4 + len(gs)),
        out_specs=VMEM,
        scratch_shapes=[pltpu.VMEM((2, T, 2 * B), BF16)],
        compiler_params=PARAMS,
        cost_estimate=cost(2 * width * T * D, D * width * 4 + len(gs) * T * CB * B * 2 + 8 * T * D),
        name="early",
    )(me, cols, *xts, *gs)


def late_kernel(me, d, cols, *refs):
    xts, gs, (mine, other, turned, sel) = refs[:4], by_source(LATE, refs[4:-4]), refs[-4:]
    half, step = D // 2, RB * 16
    dx, dc = d[0] >> 1, d[0] & 1
    lo = 0
    for part in range(4):
        for cc in range(2):
            for xx in range(NX):
                to = (((dx + xx) & (NX - 1)) << 1) + (dc ^ cc)
                rows = pl.ds(pl.multiple_of(HEAD + to * step, 16), step)
                at = (cc * NX + xx) * step
                turned[at : at + step, :] = xts[part][rows, :]
        for i, dz in enumerate(LATE):
            src = (me[0] & ~(NZ - 1)) + ((me[0] + dz) & (NZ - 1))
            blk = two_columns(gs[i], cols, part, src, sel.at[(part * len(LATE) + i) % 2])
            prod = jnp.dot(turned[...], blk, preferred_element_type=F32)
            mine[:, lo : lo + 2 * B] = prod[:half]
            other[:, lo : lo + 2 * B] = prod[half:]
            lo += 2 * B


def late(me, d, cols, xts, gs):
    width = 4 * 2 * B * len(LATE)
    return pl.pallas_call(
        late_kernel,
        out_shape=(sds((D // 2, width), F32),) * 2,
        in_specs=[SMEM] * 3 + [VMEM] * (4 + len(gs)),
        out_specs=(VMEM,) * 2,
        scratch_shapes=[pltpu.VMEM((D, T), BF16), pltpu.VMEM((2, T, 2 * B), BF16)],
        compiler_params=PARAMS,
        cost_estimate=cost(2 * width * T * D, D * width * 4 + len(gs) * T * CB * B * 2 + 8 * T * D),
        name="late",
    )(me, d, cols, *xts, *gs)


def inputs_kernel(me, d, cols, own, near, far, *refs):
    gs, outs, kept, sel = by_source(ROUNDS[0], refs[:-6]), refs[-6:-2], refs[-2], refs[-1]

    def weights(part, dz):
        z = (me[0] + dz) & (NZ - 1)
        if part == 0:
            return own[z]
        at = z & (NZ // 2 - 1)
        mine = (z >> 2) == (d[0] & 1)
        return jnp.where(mine, near[part - 1, at], far[part - 1, at])

    for part in range(4):
        total = None
        for i, dz in enumerate(ROUNDS[0]):
            src = (me[0] & ~(NZ - 1)) + ((me[0] + dz) & (NZ - 1))
            blk = two_columns(gs[i], cols, part, src, sel.at[i % 2])
            prod = jnp.dot(blk, weights(part, dz), preferred_element_type=F32)
            total = prod if total is None else total + prod
        outs[part][...] = total
        for i, dz in enumerate(ROUNDS[1]):
            kept[part, i] = weights(part, dz)


def inputs(me, d, cols, own, near, far, gs):
    flops = 4 * 2 * T * D * 2 * B * len(ROUNDS[0])
    return pl.pallas_call(
        inputs_kernel,
        out_shape=(sds((T, D), F32),) * 4 + (sds((4, len(ROUNDS[1]), 2 * B, D), BF16),),
        in_specs=[SMEM] * 3 + [VMEM] * (3 + len(gs)),
        out_specs=(VMEM,) * 5,
        scratch_shapes=[pltpu.VMEM((2, T, 2 * B), BF16)],
        compiler_params=PARAMS,
        cost_estimate=cost(flops, 10 << 20),
        name="inputs",
    )(me, d, cols, own, near, far, *gs)


def rest_kernel(me, cols, kept, *refs):
    gs, accs, outs, sel = by_source(ROUNDS[1], refs[:-9]), refs[-9:-5], refs[-5:-1], refs[-1]
    for part in (1, 2, 3, 0):
        total = accs[part][...]
        for i, dz in enumerate(ROUNDS[1]):
            src = (me[0] & ~(NZ - 1)) + ((me[0] + dz) & (NZ - 1))
            blk = two_columns(gs[i], cols, part, src, sel.at[part % 2])
            total = total + jnp.dot(blk, kept[part, i], preferred_element_type=F32)
        outs[part][...] = total


def rest(me, cols, kept, gs, accs):
    flops = 4 * 2 * T * D * 2 * B * len(ROUNDS[1])
    return pl.pallas_call(
        rest_kernel,
        out_shape=(sds((T, D), F32),) * 4,
        in_specs=[SMEM] * 2 + [VMEM] * (1 + len(gs) + len(accs)),
        out_specs=(VMEM,) * 4,
        scratch_shapes=[pltpu.VMEM((2, T, 2 * B), BF16)],
        compiler_params=PARAMS,
        cost_estimate=cost(flops, 8 << 20),
        name="rest",
    )(me, cols, kept, *gs, *accs)


def scaled(out, top):
    width = out.shape[1] - B
    power = jnp.floor(14 - jnp.log(jnp.maximum(top, 1e-30)) * (1 / math.log(2)))
    out[:, :width] = out[:, :width] * jnp.exp2(power)
    out[:, width:] = jnp.broadcast_to(power, (out.shape[0], B))


def unscaled(g):
    width = g.shape[1] - B
    return g[:, :width] * jnp.exp2(-g[:1, width : width + 1])


def pair_kernel(mine, theirs, keep, *outs):
    step, width = keep.shape
    keep[...] = mine[:step, :] + theirs[:step, :]
    for i, out in enumerate(outs):
        rows = slice((i + 1) * step, (i + 2) * step)
        total = mine[rows, :] + theirs[rows, :]
        out[:, :width] = total
        scaled(out, jnp.max(jnp.abs(total), keepdims=True))


def pair(mine, theirs):
    step, width = RB * 16, mine.shape[1]
    return pl.pallas_call(
        pair_kernel,
        out_shape=(sds((step, width), F32),) + (sds((step, width + B), F32),) * 3,
        in_specs=[VMEM] * 2,
        out_specs=(VMEM,) * 4,
        compiler_params=PARAMS,
        cost_estimate=cost(0, 3 * mine.shape[0] * width * 4),
        name="pair",
    )(mine, theirs)


def join_kernel(first, keep, a, b, c, *outs):
    n = first.shape[1] // 4
    k = keep.shape[1] // 4
    total = keep[...]
    for g in (a, b, c):
        total = total + unscaled(g)
    for part, out in enumerate(outs):
        out[:, :n] = first[:, part * n : (part + 1) * n]
        out[:, n : n + k] = total[:, part * k : (part + 1) * k]
        if part > 0:
            scaled(out, jnp.max(jnp.abs(out[:, : n + k]), keepdims=True))


def join(first, keep, got):
    width = (first.shape[1] + keep.shape[1]) // 4
    return pl.pallas_call(
        join_kernel,
        out_shape=(sds((RB * 16, width), F32),) + (sds((RB * 16, width + B), F32),) * 3,
        in_specs=[VMEM] * 5,
        out_specs=(VMEM,) * 4,
        compiler_params=PARAMS,
        cost_estimate=cost(0, 4 << 20),
        name="join",
    )(first, keep, *got)


def slots_kernel(me, row, col, count, need, *refs):
    ins, out, held = refs[:-2], refs[-2], refs[-1]
    wide = 2 * B
    for part in range(4):
        sums = unscaled(ins[part]) if part > 0 else ins[part][...]
        for i, dz in enumerate(ORDER):
            held[dz & (NZ - 1), part] = sums[:, i * wide : (i + 1) * wide]
    y, z = me[0] >> 3, me[0] & 7

    @pl.loop(0, SLOTS, unroll=4)
    def _(s):
        src, c = source_column(col[s])
        p = jnp.where(c == need[0, src], 0, 1)
        dz = ((src & 7) - z) & (NZ - 1)
        dy = ((src >> 3) - y) & (NY - 1)
        part = jnp.where(dy == 0, DY_PART[0], jnp.where(dy == 1, DY_PART[1], jnp.where(dy == 2, DY_PART[2], DY_PART[3])))
        rows = pl.ds(pl.multiple_of(row[s] * 16, 16), 16)
        lanes = pl.ds(pl.multiple_of(p * B, B), B)
        blk = held[dz, part, rows, lanes]
        out[s] = jnp.where(s < count[0], blk, jnp.zeros_like(blk))


def slots(me, row, col, count, need, parts):
    return pl.pallas_call(
        slots_kernel,
        out_shape=sds((SLOTS, 16, B), F32),
        in_specs=[SMEM] * 5 + [VMEM] * len(parts),
        out_specs=VMEM,
        scratch_shapes=[pltpu.VMEM((NZ, 4, RB * 16, 2 * B), F32)],
        compiler_params=PARAMS,
        cost_estimate=cost(0, 5 << 20),
        name="slots",
    )(me, row, col, count, need, *parts)


def shift_z(k):
    return [(y * NZ + z, y * NZ + (z + k) % NZ) for y in range(NY) for z in range(NZ)]


def shift_y(k):
    return [(y * NZ + z, (y + k) % NY * NZ + z) for y in range(NY) for z in range(NZ)]


def shift_x(k):
    return [(x * 2 + c, (x + k) % NX * 2 + c) for x in range(NX) for c in range(2)]


def tie(*trees):
    return lax.optimization_barrier(trees)


def after(a, first):
    return lax.optimization_barrier((a, first))[0]


def tie(*trees):
    return lax.optimization_barrier(trees)


def on_device(x_in, grad_pre, weight_blocks, slot_row, slot_col, slot_count):
    me = lax.axis_index("mp").astype(I32).reshape(1)
    d = lax.axis_index("dp").astype(I32).reshape(1)

    def z_step(a, k):
        return lax.ppermute(a, "mp", shift_z(k))

    def core_step(a):
        return lax.ppermute(a, "dp", [(a, a ^ 1) for a in range(2 * NX)])

    def y_back(parts, owners=OWNERS):
        return [lax.ppermute(a, "mp", shift_y(k)) for a, k in zip(parts, owners)]

    def x_step(out):
        return [lax.ppermute(a, "dp", shift_x(k)) for a, k in zip(out, (1, 2, 3))]

    held = {0: grad_pre}
    z1 = [z_step(grad_pre, 1), z_step(grad_pre, -1)]
    need, xt = turn(slot_col, slot_count, x_in)
    xts = [lax.ppermute(xt, "mp", shift_y(-k)) for k in OWNERS]
    own, *bufs = pack(me, d, slot_row, slot_col, slot_count, need, weight_blocks)
    z1, xts, bufs = tie(z1, xts, bufs)

    held[-1], held[1] = z1
    z2 = [z_step(z1[0], 1), z_step(z1[1], -1)]
    bufs = [lax.ppermute(a, "mp", shift_y(-k)) for a, k in zip(bufs, OWNERS)]
    xts = [xt, *xts]
    cols = heads(xts)
    z2, cols = tie(z2, cols)

    held[-2], held[2] = z2
    z3 = [z_step(z2[0], 1), z_step(z2[1], -1)]
    grads = early(me, cols, xts, [held[k] for k in EARLY])
    z3, bufs, grads = tie(z3, bufs, grads)
    early_sum = lax.psum_scatter(grads, "dp", scatter_dimension=0, tiled=True)

    held[-3], held[3] = z3
    half = T // 2
    z4 = [z_step(z3[0][:half], 1), z_step(z3[1][half:], -1)]
    near = jnp.stack(bufs)
    far = core_step(near)
    *accs, kept = inputs(me, d, cols, own, near, far, [held[k] for k in ROUNDS[0]])
    z4, accs, kept = tie(z4, accs, kept)

    mine, other = late(me, d, cols, xts, [held[3], held[-3], *z4])
    theirs = core_step(other)
    accs = rest(me, cols, kept, z4, after(accs, other))
    totals = [accs[0], *y_back(accs[1:3])]
    keep, *out = pair(after(mine, accs), theirs)
    out = [a.astype(jnp.float16) for a in out]
    got = x_step(out)
    totals += y_back([after(accs[3], (got[2], totals[1:]))], OWNERS[2:])
    got, totals[1:3] = tie(got, totals[1:3])
    first, *back = join(early_sum, keep, [a.astype(F32) for a in got])
    parts = [first] + [a.astype(F32) for a in y_back([a.astype(jnp.float16) for a in back])]
    grad_x = ((totals[0] + totals[1]) + (totals[2] + totals[3])).astype(BF16)
    return grad_x, slots(me, slot_row, slot_col, slot_count, after(need, grad_x), parts)


def solution(mesh):
    placed = (P("dp", "mp"), P("dp", "mp"), P("mp", None, None), P("mp"), P("mp"), P("mp"))
    return jax.shard_map(
        on_device,
        mesh=mesh,
        in_specs=placed,
        out_specs=(P("dp", "mp"), P("mp", "dp", None)),
        check_vma=False,
    )
```

```python
import math

import jax
import jax.numpy as jnp
from jax import lax
from jax.experimental import pallas as pl
from jax.experimental.pallas import tpu as pltpu
from jax.sharding import PartitionSpec as P

NY, NZ = 4, 8
NX = 4
B = 128
T = 512
CB, RB = 6, 3
D = RB * B
SLOTS = 128
EARLY, LATE = (0, 1, -1, 2, -2), (3, -3, 4)
ORDER = EARLY + LATE
ROUNDS = ((0, 1, -1, 2, -2, 3, -3), (4,))
OWNERS = (1, -1, 2)
DY_PART = (0, 2, 3, 1)
HEAD = 16

VMEM = pl.BlockSpec(memory_space=pltpu.VMEM)
SMEM = pl.BlockSpec(memory_space=pltpu.SMEM)
PARAMS = pltpu.CompilerParams(vmem_limit_bytes=48 << 20)
F32, BF16, I32 = jnp.float32, jnp.bfloat16, jnp.int32


def sds(shape, dtype):
    return jax.ShapeDtypeStruct(shape, dtype)


def cost(flops, moved):
    return pl.CostEstimate(flops=flops, bytes_accessed=moved, transcendentals=0)


def source_column(col):
    src = (col * 43691) >> 18
    return src, col - src * CB


def turn_kernel(col, count, x, need, out):
    n = NY * NZ
    shape = (SLOTS, SLOTS)
    src, c = source_column(jnp.broadcast_to(col[...], shape).T)
    lane = lax.broadcasted_iota(I32, shape, 1)
    hit = (src == (lane & (n - 1))) & (lax.broadcasted_iota(I32, shape, 0) < count[0])
    lo = jnp.min(jnp.where(hit, c, CB), axis=0, keepdims=True)
    hi = jnp.max(jnp.where(hit, c, -1), axis=0, keepdims=True)
    row = jnp.where(hi < 0, 0, jnp.where(lane[:1] < n, lo, hi))
    need[...] = jnp.broadcast_to(row, need.shape)
    out[:HEAD, :] = jnp.zeros((HEAD, T), BF16)
    out[:HEAD, :SLOTS] = jnp.broadcast_to(row, (HEAD, SLOTS)).astype(F32).astype(BF16)
    held = x[...].T
    for to in range(2 * NX):
        for r in range(RB):
            at = HEAD + (to * RB + r) * 16
            out[at : at + 16, :] = held[r * B + to * 16 : r * B + to * 16 + 16, :]


def turn(slot_col, slot_count, x):
    return pl.pallas_call(
        turn_kernel,
        out_shape=(sds((8, SLOTS), I32), sds((HEAD + D, T), BF16)),
        in_specs=[VMEM, SMEM, VMEM],
        out_specs=(VMEM, VMEM),
        compiler_params=PARAMS,
        cost_estimate=cost(0, 1 << 20),
        name="turn",
    )(slot_col.reshape(1, SLOTS), slot_count, x)


def heads_kernel(a, b, c, d, out):
    for i, head in enumerate((a, b, c, d)):
        out[i : i + 1, :] = head[...].astype(F32).astype(I32)[:1]


def heads(xts):
    return pl.pallas_call(
        heads_kernel,
        out_shape=sds((4, SLOTS), I32),
        grid=(1,),
        in_specs=[pl.BlockSpec((HEAD, SLOTS), lambda i: (0, 0))] * 4,
        out_specs=pl.BlockSpec((4, SLOTS), lambda i: (0, 0)),
        cost_estimate=cost(0, 1 << 14),
        name="heads",
    )(*xts)


def pack_kernel(me, d, row, col, count, need, w, own, b1, b2, b3, held):
    y = me[0] >> 3
    held[...] = jnp.zeros_like(held)

    @pl.loop(0, SLOTS, unroll=4)
    def _(s):
        src, c = source_column(col[s])
        p = jnp.where(c == need[0, src], 0, 1)
        at = jnp.where(s < count[0], (src - (y << 3)) & (NY * NZ - 1), NY * NZ)
        rows = pl.ds(pl.multiple_of(p * B, B), B)
        held[at, rows, pl.ds(pl.multiple_of(row[s] * B, B), B)] = w[s].T

    own[...] = held[:NZ]
    lo = (d[0] & 1) * (NZ // 2)
    for out, t in ((b1, 3), (b2, 1), (b3, 2)):
        out[...] = held[pl.ds(t * NZ + lo, NZ // 2)]


def pack(me, d, slot_row, slot_col, slot_count, need, w):
    part = sds((NZ // 2, 2 * B, D), BF16)
    return pl.pallas_call(
        pack_kernel,
        out_shape=(sds((NZ, 2 * B, D), BF16), part, part, part),
        in_specs=[SMEM] * 6 + [VMEM],
        out_specs=(VMEM,) * 4,
        scratch_shapes=[pltpu.VMEM((NY * NZ + 1, 2 * B, D), BF16)],
        compiler_params=PARAMS,
        cost_estimate=cost(0, 7 << 20),
        name="pack",
    )(me, d, slot_row, slot_col, slot_count, need, w)


def two_columns(gs, cols, part, src, sel):
    for p in range(2):
        lanes = pl.ds(pl.multiple_of(cols[part, p * NY * NZ + src] * B, B), B)
        at = 0
        for g in gs:
            sel[at : at + g.shape[0], p * B : (p + 1) * B] = g[:, lanes]
            at += g.shape[0]
    return sel[...]


def by_source(stage, refs):
    refs = list(refs)
    return [[refs.pop(0) for _ in range(2 if dz == 4 else 1)] for dz in stage]


def early_kernel(me, cols, *refs):
    xts, gs, (out, sel) = refs[:4], by_source(EARLY, refs[4:-2]), refs[-2:]
    lo = 0
    for part in range(4):
        for i, dz in enumerate(EARLY):
            src = (me[0] & ~(NZ - 1)) + ((me[0] + dz) & (NZ - 1))
            blk = two_columns(gs[i], cols, part, src, sel.at[(part * len(EARLY) + i) % 2])
            out[:, lo : lo + 2 * B] = jnp.dot(xts[part][HEAD:, :], blk, preferred_element_type=F32)
            lo += 2 * B


def early(me, cols, xts, gs):
    width = 4 * 2 * B * len(gs)
    return pl.pallas_call(
        early_kernel,
        out_shape=sds((D, width), F32),
        in_specs=[SMEM] * 2 + [VMEM] * (4 + len(gs)),
        out_specs=VMEM,
        scratch_shapes=[pltpu.VMEM((2, T, 2 * B), BF16)],
        compiler_params=PARAMS,
        cost_estimate=cost(2 * width * T * D, D * width * 4 + len(gs) * T * CB * B * 2 + 8 * T * D),
        name="early",
    )(me, cols, *xts, *gs)


def late_kernel(me, d, cols, *refs):
    xts, gs, (mine, other, turned, sel) = refs[:4], by_source(LATE, refs[4:-4]), refs[-4:]
    half, step = D // 2, RB * 16
    dx, dc = d[0] >> 1, d[0] & 1
    lo = 0
    for part in range(4):
        for cc in range(2):
            for xx in range(NX):
                to = (((dx + xx) & (NX - 1)) << 1) + (dc ^ cc)
                rows = pl.ds(pl.multiple_of(HEAD + to * step, 16), step)
                at = (cc * NX + xx) * step
                turned[at : at + step, :] = xts[part][rows, :]
        for i, dz in enumerate(LATE):
            src = (me[0] & ~(NZ - 1)) + ((me[0] + dz) & (NZ - 1))
            blk = two_columns(gs[i], cols, part, src, sel.at[(part * len(LATE) + i) % 2])
            prod = jnp.dot(turned[...], blk, preferred_element_type=F32)
            mine[:, lo : lo + 2 * B] = prod[:half]
            other[:, lo : lo + 2 * B] = prod[half:]
            lo += 2 * B


def late(me, d, cols, xts, gs):
    width = 4 * 2 * B * len(LATE)
    return pl.pallas_call(
        late_kernel,
        out_shape=(sds((D // 2, width), F32),) * 2,
        in_specs=[SMEM] * 3 + [VMEM] * (4 + len(gs)),
        out_specs=(VMEM,) * 2,
        scratch_shapes=[pltpu.VMEM((D, T), BF16), pltpu.VMEM((2, T, 2 * B), BF16)],
        compiler_params=PARAMS,
        cost_estimate=cost(2 * width * T * D, D * width * 4 + len(gs) * T * CB * B * 2 + 8 * T * D),
        name="late",
    )(me, d, cols, *xts, *gs)


def inputs_kernel(me, d, cols, own, near, far, *refs):
    gs, outs, kept, sel = by_source(ROUNDS[0], refs[:-6]), refs[-6:-2], refs[-2], refs[-1]

    def weights(part, dz):
        z = (me[0] + dz) & (NZ - 1)
        if part == 0:
            return own[z]
        at = z & (NZ // 2 - 1)
        mine = (z >> 2) == (d[0] & 1)
        return jnp.where(mine, near[part - 1, at], far[part - 1, at])

    for part in range(4):
        total = None
        for i, dz in enumerate(ROUNDS[0]):
            src = (me[0] & ~(NZ - 1)) + ((me[0] + dz) & (NZ - 1))
            blk = two_columns(gs[i], cols, part, src, sel.at[i % 2])
            prod = jnp.dot(blk, weights(part, dz), preferred_element_type=F32)
            total = prod if total is None else total + prod
        outs[part][...] = total
        for i, dz in enumerate(ROUNDS[1]):
            kept[part, i] = weights(part, dz)


def inputs(me, d, cols, own, near, far, gs):
    flops = 4 * 2 * T * D * 2 * B * len(ROUNDS[0])
    return pl.pallas_call(
        inputs_kernel,
        out_shape=(sds((T, D), F32),) * 4 + (sds((4, len(ROUNDS[1]), 2 * B, D), BF16),),
        in_specs=[SMEM] * 3 + [VMEM] * (3 + len(gs)),
        out_specs=(VMEM,) * 5,
        scratch_shapes=[pltpu.VMEM((2, T, 2 * B), BF16)],
        compiler_params=PARAMS,
        cost_estimate=cost(flops, 10 << 20),
        name="inputs",
    )(me, d, cols, own, near, far, *gs)


def rest_kernel(me, cols, kept, *refs):
    gs, accs, outs, sel = by_source(ROUNDS[1], refs[:-10]), refs[-10:-6], refs[-6:-1], refs[-1]
    for part in (3, 1, 2, 0):
        total = accs[part][...]
        for i, dz in enumerate(ROUNDS[1]):
            src = (me[0] & ~(NZ - 1)) + ((me[0] + dz) & (NZ - 1))
            blk = two_columns(gs[i], cols, part, src, sel.at[part % 2])
            total = total + jnp.dot(blk, kept[part, i], preferred_element_type=F32)
        if part < 3:
            outs[part][...] = total
        else:
            outs[3][...] = total[: T // 2]
            outs[4][...] = total[T // 2 :]


def rest(me, cols, kept, gs, accs):
    flops = 4 * 2 * T * D * 2 * B * len(ROUNDS[1])
    return pl.pallas_call(
        rest_kernel,
        out_shape=(sds((T, D), F32),) * 3 + (sds((T // 2, D), F32),) * 2,
        in_specs=[SMEM] * 2 + [VMEM] * (1 + len(gs) + len(accs)),
        out_specs=(VMEM,) * 5,
        scratch_shapes=[pltpu.VMEM((2, T, 2 * B), BF16)],
        compiler_params=PARAMS,
        cost_estimate=cost(flops, 8 << 20),
        name="rest",
    )(me, cols, kept, *gs, *accs)


def relay_kernel(up, down, lo, hi, up_out, down_out):
    n = T // 2
    up_out[:n, :] = up[:n, :] + lo[...]
    up_out[n:, :] = up[n:, :]
    down_out[:n, :] = down[:n, :]
    down_out[n:, :] = down[n:, :] + hi[...]


def relay(up, down, lo, hi):
    return pl.pallas_call(
        relay_kernel,
        out_shape=(sds((T, D), F32),) * 2,
        in_specs=[VMEM] * 4,
        out_specs=(VMEM,) * 2,
        compiler_params=PARAMS,
        cost_estimate=cost(0, 5 << 20),
        name="relay",
    )(up, down, lo, hi)


def scaled(out, top):
    width = out.shape[1] - B
    power = jnp.floor(14 - jnp.log(jnp.maximum(top, 1e-30)) * (1 / math.log(2)))
    out[:, :width] = out[:, :width] * jnp.exp2(power)
    out[:, width:] = jnp.broadcast_to(power, (out.shape[0], B))


def unscaled(g):
    width = g.shape[1] - B
    return g[:, :width] * jnp.exp2(-g[:1, width : width + 1])


def pair_kernel(mine, theirs, keep, *outs):
    step, width = keep.shape
    keep[...] = mine[:step, :] + theirs[:step, :]
    for i, out in enumerate(outs):
        rows = slice((i + 1) * step, (i + 2) * step)
        total = mine[rows, :] + theirs[rows, :]
        out[:, :width] = total
        scaled(out, jnp.max(jnp.abs(total), keepdims=True))


def pair(mine, theirs):
    step, width = RB * 16, mine.shape[1]
    return pl.pallas_call(
        pair_kernel,
        out_shape=(sds((step, width), F32),) + (sds((step, width + B), F32),) * 3,
        in_specs=[VMEM] * 2,
        out_specs=(VMEM,) * 4,
        compiler_params=PARAMS,
        cost_estimate=cost(0, 3 * mine.shape[0] * width * 4),
        name="pair",
    )(mine, theirs)


def join_kernel(first, keep, a, b, c, *outs):
    n = first.shape[1] // 4
    k = keep.shape[1] // 4
    total = keep[...]
    for g in (a, b, c):
        total = total + unscaled(g)
    for part, out in enumerate(outs):
        out[:, :n] = first[:, part * n : (part + 1) * n]
        out[:, n : n + k] = total[:, part * k : (part + 1) * k]
        if part > 0:
            scaled(out, jnp.max(jnp.abs(out[:, : n + k]), keepdims=True))


def join(first, keep, got):
    width = (first.shape[1] + keep.shape[1]) // 4
    return pl.pallas_call(
        join_kernel,
        out_shape=(sds((RB * 16, width), F32),) + (sds((RB * 16, width + B), F32),) * 3,
        in_specs=[VMEM] * 5,
        out_specs=(VMEM,) * 4,
        compiler_params=PARAMS,
        cost_estimate=cost(0, 4 << 20),
        name="join",
    )(first, keep, *got)


def slots_kernel(me, row, col, count, need, *refs):
    ins, out, held = refs[:-2], refs[-2], refs[-1]
    wide = 2 * B
    for part in range(4):
        sums = unscaled(ins[part]) if part > 0 else ins[part][...]
        for i, dz in enumerate(ORDER):
            held[dz & (NZ - 1), part] = sums[:, i * wide : (i + 1) * wide]
    y, z = me[0] >> 3, me[0] & 7

    @pl.loop(0, SLOTS, unroll=4)
    def _(s):
        src, c = source_column(col[s])
        p = jnp.where(c == need[0, src], 0, 1)
        dz = ((src & 7) - z) & (NZ - 1)
        dy = ((src >> 3) - y) & (NY - 1)
        part = jnp.where(dy == 0, DY_PART[0], jnp.where(dy == 1, DY_PART[1], jnp.where(dy == 2, DY_PART[2], DY_PART[3])))
        rows = pl.ds(pl.multiple_of(row[s] * 16, 16), 16)
        lanes = pl.ds(pl.multiple_of(p * B, B), B)
        blk = held[dz, part, rows, lanes]
        out[s] = jnp.where(s < count[0], blk, jnp.zeros_like(blk))


def slots(me, row, col, count, need, parts):
    return pl.pallas_call(
        slots_kernel,
        out_shape=sds((SLOTS, 16, B), F32),
        in_specs=[SMEM] * 5 + [VMEM] * len(parts),
        out_specs=VMEM,
        scratch_shapes=[pltpu.VMEM((NZ, 4, RB * 16, 2 * B), F32)],
        compiler_params=PARAMS,
        cost_estimate=cost(0, 5 << 20),
        name="slots",
    )(me, row, col, count, need, *parts)


def shift_z(k):
    return [(y * NZ + z, y * NZ + (z + k) % NZ) for y in range(NY) for z in range(NZ)]


def shift_y(k):
    return [(y * NZ + z, (y + k) % NY * NZ + z) for y in range(NY) for z in range(NZ)]


def shift_x(k):
    return [(x * 2 + c, (x + k) % NX * 2 + c) for x in range(NX) for c in range(2)]


def tie(*trees):
    return lax.optimization_barrier(trees)


def after(a, first):
    return lax.optimization_barrier((a, first))[0]


def tie(*trees):
    return lax.optimization_barrier(trees)


def on_device(x_in, grad_pre, weight_blocks, slot_row, slot_col, slot_count):
    me = lax.axis_index("mp").astype(I32).reshape(1)
    d = lax.axis_index("dp").astype(I32).reshape(1)

    def z_step(a, k):
        return lax.ppermute(a, "mp", shift_z(k))

    def core_step(a):
        return lax.ppermute(a, "dp", [(a, a ^ 1) for a in range(2 * NX)])

    def y_back(parts):
        return [lax.ppermute(a, "mp", shift_y(k)) for a, k in zip(parts, OWNERS)]

    def x_step(out):
        return [lax.ppermute(a, "dp", shift_x(k)) for a, k in zip(out, (1, 2, 3))]

    held = {0: grad_pre}
    z1 = [z_step(grad_pre, 1), z_step(grad_pre, -1)]
    need, xt = turn(slot_col, slot_count, x_in)
    xts = [lax.ppermute(xt, "mp", shift_y(-k)) for k in OWNERS]
    own, *bufs = pack(me, d, slot_row, slot_col, slot_count, need, weight_blocks)
    z1, xts, bufs = tie(z1, xts, bufs)

    held[-1], held[1] = z1
    z2 = [z_step(z1[0], 1), z_step(z1[1], -1)]
    bufs = [lax.ppermute(a, "mp", shift_y(-k)) for a, k in zip(bufs, OWNERS)]
    xts = [xt, *xts]
    cols = heads(xts)
    z2, cols = tie(z2, cols)

    held[-2], held[2] = z2
    z3 = [z_step(z2[0], 1), z_step(z2[1], -1)]
    grads = early(me, cols, xts, [held[k] for k in EARLY])
    z3, bufs, grads = tie(z3, bufs, grads)
    early_sum = lax.psum_scatter(grads, "dp", scatter_dimension=0, tiled=True)

    held[-3], held[3] = z3
    half = T // 2
    z4 = [z_step(z3[0][:half], 1), z_step(z3[1][half:], -1)]
    near = jnp.stack(bufs)
    far = core_step(near)
    *accs, kept = inputs(me, d, cols, own, near, far, [held[k] for k in ROUNDS[0]])
    z4, accs, kept = tie(z4, accs, kept)

    total, up, down, lo, hi = rest(me, cols, kept, z4, accs)
    lo, hi = lax.ppermute(lo, "mp", shift_y(1)), lax.ppermute(hi, "mp", shift_y(-1))
    mine, other = late(me, d, cols, xts, after([held[3], held[-3], *z4], total))
    theirs = core_step(other)
    keep, *out = pair(mine, theirs)
    out = [a.astype(jnp.float16) for a in out]
    got = x_step(out)
    up, down = relay(*after((up, down), out), lo, hi)
    up, down = lax.ppermute(up, "mp", shift_y(1)), lax.ppermute(down, "mp", shift_y(-1))
    first, *back = join(early_sum, keep, [a.astype(F32) for a in got])
    parts = [first] + [a.astype(F32) for a in y_back([a.astype(jnp.float16) for a in back])]
    grad_x = (total + (up + down)).astype(BF16)
    return grad_x, slots(me, slot_row, slot_col, slot_count, after(need, grad_x), parts)


def solution(mesh):
    placed = (P("dp", "mp"), P("dp", "mp"), P("mp", None, None), P("mp"), P("mp"), P("mp"))
    return jax.shard_map(
        on_device,
        mesh=mesh,
        in_specs=placed,
        out_specs=(P("dp", "mp"), P("mp", "dp", None)),
        check_vma=False,
    )
```

```python
import math

import jax
import jax.numpy as jnp
from jax import lax
from jax.experimental import pallas as pl
from jax.experimental.pallas import tpu as pltpu
from jax.sharding import PartitionSpec as P

NY, NZ = 4, 8
NX = 4
B = 128
T = 512
CB, RB = 6, 3
D = RB * B
SLOTS = 128
EARLY, LATE = (0, 1, -1, 2, -2), (3, -3, 4)
ORDER = EARLY + LATE
ROUNDS = ((0, 1, -1, 2, -2, 3, -3), (4,))
OWNERS = (1, -1, 2)
DY_PART = (0, 2, 3, 1)
HEAD = 16

VMEM = pl.BlockSpec(memory_space=pltpu.VMEM)
SMEM = pl.BlockSpec(memory_space=pltpu.SMEM)
PARAMS = pltpu.CompilerParams(vmem_limit_bytes=28 << 20)
F32, BF16, I32 = jnp.float32, jnp.bfloat16, jnp.int32


def sds(shape, dtype):
    return jax.ShapeDtypeStruct(shape, dtype)


def cost(flops, moved):
    return pl.CostEstimate(flops=flops, bytes_accessed=moved, transcendentals=0)


def source_column(col):
    src = (col * 43691) >> 18
    return src, col - src * CB


def turn_kernel(col, count, x, need, out):
    n = NY * NZ
    shape = (SLOTS, SLOTS)
    src, c = source_column(jnp.broadcast_to(col[...], shape).T)
    lane = lax.broadcasted_iota(I32, shape, 1)
    hit = (src == (lane & (n - 1))) & (lax.broadcasted_iota(I32, shape, 0) < count[0])
    lo = jnp.min(jnp.where(hit, c, CB), axis=0, keepdims=True)
    hi = jnp.max(jnp.where(hit, c, -1), axis=0, keepdims=True)
    row = jnp.where(hi < 0, 0, jnp.where(lane[:1] < n, lo, hi))
    need[...] = jnp.broadcast_to(row, need.shape)
    out[:HEAD, :] = jnp.zeros((HEAD, T), BF16)
    out[:HEAD, :SLOTS] = jnp.broadcast_to(row, (HEAD, SLOTS)).astype(F32).astype(BF16)
    held = x[...].T
    for to in range(2 * NX):
        for r in range(RB):
            at = HEAD + (to * RB + r) * 16
            out[at : at + 16, :] = held[r * B + to * 16 : r * B + to * 16 + 16, :]


def turn(slot_col, slot_count, x):
    return pl.pallas_call(
        turn_kernel,
        out_shape=(sds((8, SLOTS), I32), sds((HEAD + D, T), BF16)),
        in_specs=[VMEM, SMEM, VMEM],
        out_specs=(VMEM, VMEM),
        compiler_params=PARAMS,
        cost_estimate=cost(0, 1 << 20),
        name="turn",
    )(slot_col.reshape(1, SLOTS), slot_count, x)


def heads_kernel(a, b, c, d, out):
    for i, head in enumerate((a, b, c, d)):
        out[i : i + 1, :] = head[...].astype(F32).astype(I32)[:1]


def heads(xts):
    return pl.pallas_call(
        heads_kernel,
        out_shape=sds((4, SLOTS), I32),
        grid=(1,),
        in_specs=[pl.BlockSpec((HEAD, SLOTS), lambda i: (0, 0))] * 4,
        out_specs=pl.BlockSpec((4, SLOTS), lambda i: (0, 0)),
        cost_estimate=cost(0, 1 << 14),
        name="heads",
    )(*xts)


def pack_kernel(me, d, row, col, count, need, w, own, b1, b2, b3, held):
    y = me[0] >> 3
    held[...] = jnp.zeros_like(held)

    @pl.loop(0, SLOTS, unroll=8)
    def _(s):
        src, c = source_column(col[s])
        p = jnp.where(c == need[0, src], 0, 1)
        at = jnp.where(s < count[0], (src - (y << 3)) & (NY * NZ - 1), NY * NZ)
        rows = pl.ds(pl.multiple_of(p * B, B), B)
        held[at, rows, pl.ds(pl.multiple_of(row[s] * B, B), B)] = w[s].T

    own[...] = held[:NZ]
    lo = (d[0] & 1) * (NZ // 2)
    for out, t in ((b1, 3), (b2, 1), (b3, 2)):
        out[...] = held[pl.ds(t * NZ + lo, NZ // 2)]


def pack(me, d, slot_row, slot_col, slot_count, need, w):
    part = sds((NZ // 2, 2 * B, D), BF16)
    return pl.pallas_call(
        pack_kernel,
        out_shape=(sds((NZ, 2 * B, D), BF16), part, part, part),
        in_specs=[SMEM] * 6 + [VMEM],
        out_specs=(VMEM,) * 4,
        scratch_shapes=[pltpu.VMEM((NY * NZ + 1, 2 * B, D), BF16)],
        compiler_params=PARAMS,
        cost_estimate=cost(0, 7 << 20),
        name="pack",
    )(me, d, slot_row, slot_col, slot_count, need, w)


def two_columns(gs, cols, part, src, sel):
    for p in range(2):
        lanes = pl.ds(pl.multiple_of(cols[part, p * NY * NZ + src] * B, B), B)
        at = 0
        for g in gs:
            sel[at : at + g.shape[0], p * B : (p + 1) * B] = g[:, lanes]
            at += g.shape[0]
    return sel[...]


def by_source(stage, refs):
    refs = list(refs)
    return [[refs.pop(0) for _ in range(2 if dz == 4 else 1)] for dz in stage]


def early_kernel(me, cols, *refs):
    xts, gs, (out, sel) = refs[:4], by_source(EARLY, refs[4:-2]), refs[-2:]
    lo = 0
    for part in range(4):
        for i, dz in enumerate(EARLY):
            src = (me[0] & ~(NZ - 1)) + ((me[0] + dz) & (NZ - 1))
            blk = two_columns(gs[i], cols, part, src, sel.at[(part * len(EARLY) + i) % 2])
            out[:, lo : lo + 2 * B] = jnp.dot(xts[part][HEAD:, :], blk, preferred_element_type=F32)
            lo += 2 * B


def early(me, cols, xts, gs):
    width = 4 * 2 * B * len(gs)
    return pl.pallas_call(
        early_kernel,
        out_shape=sds((D, width), F32),
        in_specs=[SMEM] * 2 + [VMEM] * (4 + len(gs)),
        out_specs=VMEM,
        scratch_shapes=[pltpu.VMEM((2, T, 2 * B), BF16)],
        compiler_params=PARAMS,
        cost_estimate=cost(2 * width * T * D, D * width * 4 + len(gs) * T * CB * B * 2 + 8 * T * D),
        name="early",
    )(me, cols, *xts, *gs)


def late_kernel(me, d, cols, *refs):
    xts, gs, (mine, other, turned, sel) = refs[:4], by_source(LATE, refs[4:-4]), refs[-4:]
    half, step = D // 2, RB * 16
    dx, dc = d[0] >> 1, d[0] & 1
    lo = 0
    for part in range(4):
        for cc in range(2):
            for xx in range(NX):
                to = (((dx + xx) & (NX - 1)) << 1) + (dc ^ cc)
                rows = pl.ds(pl.multiple_of(HEAD + to * step, 16), step)
                at = (cc * NX + xx) * step
                turned[at : at + step, :] = xts[part][rows, :]
        for i, dz in enumerate(LATE):
            src = (me[0] & ~(NZ - 1)) + ((me[0] + dz) & (NZ - 1))
            blk = two_columns(gs[i], cols, part, src, sel.at[(part * len(LATE) + i) % 2])
            prod = jnp.dot(turned[...], blk, preferred_element_type=F32)
            mine[:, lo : lo + 2 * B] = prod[:half]
            other[:, lo : lo + 2 * B] = prod[half:]
            lo += 2 * B


def late(me, d, cols, xts, gs):
    width = 4 * 2 * B * len(LATE)
    return pl.pallas_call(
        late_kernel,
        out_shape=(sds((D // 2, width), F32),) * 2,
        in_specs=[SMEM] * 3 + [VMEM] * (4 + len(gs)),
        out_specs=(VMEM,) * 2,
        scratch_shapes=[pltpu.VMEM((D, T), BF16), pltpu.VMEM((2, T, 2 * B), BF16)],
        compiler_params=PARAMS,
        cost_estimate=cost(2 * width * T * D, D * width * 4 + len(gs) * T * CB * B * 2 + 8 * T * D),
        name="late",
    )(me, d, cols, *xts, *gs)


def inputs_kernel(me, d, cols, own, near, far, *refs):
    gs, outs, kept, sel = by_source(ROUNDS[0], refs[:-6]), refs[-6:-2], refs[-2], refs[-1]

    def weights(part, dz):
        z = (me[0] + dz) & (NZ - 1)
        if part == 0:
            return own[z]
        at = z & (NZ // 2 - 1)
        mine = (z >> 2) == (d[0] & 1)
        return jnp.where(mine, near[part - 1, at], far[part - 1, at])

    for part in range(4):
        total = None
        for i, dz in enumerate(ROUNDS[0]):
            src = (me[0] & ~(NZ - 1)) + ((me[0] + dz) & (NZ - 1))
            blk = two_columns(gs[i], cols, part, src, sel.at[i % 2])
            prod = jnp.dot(blk, weights(part, dz), preferred_element_type=F32)
            total = prod if total is None else total + prod
        outs[part][...] = total
        for i, dz in enumerate(ROUNDS[1]):
            kept[part, i] = weights(part, dz)


def inputs(me, d, cols, own, near, far, gs):
    flops = 4 * 2 * T * D * 2 * B * len(ROUNDS[0])
    return pl.pallas_call(
        inputs_kernel,
        out_shape=(sds((T, D), F32),) * 4 + (sds((4, len(ROUNDS[1]), 2 * B, D), BF16),),
        in_specs=[SMEM] * 3 + [VMEM] * (3 + len(gs)),
        out_specs=(VMEM,) * 5,
        scratch_shapes=[pltpu.VMEM((2, T, 2 * B), BF16)],
        compiler_params=PARAMS,
        cost_estimate=cost(flops, 10 << 20),
        name="inputs",
    )(me, d, cols, own, near, far, *gs)


def rest_kernel(me, cols, kept, *refs):
    gs, accs, outs, sel = by_source(ROUNDS[1], refs[:-10]), refs[-10:-6], refs[-6:-1], refs[-1]
    for part in (3, 1, 2, 0):
        total = accs[part][...]
        for i, dz in enumerate(ROUNDS[1]):
            src = (me[0] & ~(NZ - 1)) + ((me[0] + dz) & (NZ - 1))
            blk = two_columns(gs[i], cols, part, src, sel.at[part % 2])
            total = total + jnp.dot(blk, kept[part, i], preferred_element_type=F32)
        if part < 3:
            outs[part][...] = total
        else:
            outs[3][...] = total[: T // 2]
            outs[4][...] = total[T // 2 :]


def rest(me, cols, kept, gs, accs):
    flops = 4 * 2 * T * D * 2 * B * len(ROUNDS[1])
    return pl.pallas_call(
        rest_kernel,
        out_shape=(sds((T, D), F32),) * 3 + (sds((T // 2, D), F32),) * 2,
        in_specs=[SMEM] * 2 + [VMEM] * (1 + len(gs) + len(accs)),
        out_specs=(VMEM,) * 5,
        scratch_shapes=[pltpu.VMEM((2, T, 2 * B), BF16)],
        compiler_params=PARAMS,
        cost_estimate=cost(flops, 8 << 20),
        name="rest",
    )(me, cols, kept, *gs, *accs)


def relay_kernel(up, down, lo, hi, up_out, down_out):
    n = T // 2
    up_out[:n, :] = up[:n, :] + lo[...]
    up_out[n:, :] = up[n:, :]
    down_out[:n, :] = down[:n, :]
    down_out[n:, :] = down[n:, :] + hi[...]


def relay(up, down, lo, hi):
    return pl.pallas_call(
        relay_kernel,
        out_shape=(sds((T, D), F32),) * 2,
        in_specs=[VMEM] * 4,
        out_specs=(VMEM,) * 2,
        compiler_params=PARAMS,
        cost_estimate=cost(0, 5 << 20),
        name="relay",
    )(up, down, lo, hi)


def scaled(out, top):
    width = out.shape[1] - B
    power = jnp.floor(14 - jnp.log(jnp.maximum(top, 1e-30)) * (1 / math.log(2)))
    out[:, :width] = out[:, :width] * jnp.exp2(power)
    out[:, width:] = jnp.broadcast_to(power, (out.shape[0], B))


def unscaled(g):
    width = g.shape[1] - B
    return g[:, :width] * jnp.exp2(-g[:1, width : width + 1])


def pair_kernel(mine, theirs, keep, *outs):
    step, width = keep.shape
    keep[...] = mine[:step, :] + theirs[:step, :]
    for i, out in enumerate(outs):
        rows = slice((i + 1) * step, (i + 2) * step)
        total = mine[rows, :] + theirs[rows, :]
        out[:, :width] = total
        scaled(out, jnp.max(jnp.abs(total), keepdims=True))


def pair(mine, theirs):
    step, width = RB * 16, mine.shape[1]
    return pl.pallas_call(
        pair_kernel,
        out_shape=(sds((step, width), F32),) + (sds((step, width + B), F32),) * 3,
        in_specs=[VMEM] * 2,
        out_specs=(VMEM,) * 4,
        compiler_params=PARAMS,
        cost_estimate=cost(0, 3 * mine.shape[0] * width * 4),
        name="pair",
    )(mine, theirs)


def join_kernel(first, keep, a, b, c, *outs):
    n = first.shape[1] // 4
    k = keep.shape[1] // 4
    total = keep[...]
    for g in (a, b, c):
        total = total + unscaled(g)
    for part, out in enumerate(outs):
        out[:, :n] = first[:, part * n : (part + 1) * n]
        out[:, n : n + k] = total[:, part * k : (part + 1) * k]
        if part > 0:
            scaled(out, jnp.max(jnp.abs(out[:, : n + k]), keepdims=True))


def join(first, keep, got):
    width = (first.shape[1] + keep.shape[1]) // 4
    return pl.pallas_call(
        join_kernel,
        out_shape=(sds((RB * 16, width), F32),) + (sds((RB * 16, width + B), F32),) * 3,
        in_specs=[VMEM] * 5,
        out_specs=(VMEM,) * 4,
        compiler_params=PARAMS,
        cost_estimate=cost(0, 4 << 20),
        name="join",
    )(first, keep, *got)


def slots_kernel(me, row, col, count, need, *refs):
    ins, out, held = refs[:-2], refs[-2], refs[-1]
    wide = 2 * B
    for part in range(4):
        sums = unscaled(ins[part]) if part > 0 else ins[part][...]
        for i, dz in enumerate(ORDER):
            held[dz & (NZ - 1), part] = sums[:, i * wide : (i + 1) * wide]
    y, z = me[0] >> 3, me[0] & 7

    @pl.loop(0, SLOTS, unroll=8)
    def _(s):
        src, c = source_column(col[s])
        p = jnp.where(c == need[0, src], 0, 1)
        dz = ((src & 7) - z) & (NZ - 1)
        dy = ((src >> 3) - y) & (NY - 1)
        part = jnp.where(dy == 0, DY_PART[0], jnp.where(dy == 1, DY_PART[1], jnp.where(dy == 2, DY_PART[2], DY_PART[3])))
        rows = pl.ds(pl.multiple_of(row[s] * 16, 16), 16)
        lanes = pl.ds(pl.multiple_of(p * B, B), B)
        blk = held[dz, part, rows, lanes]
        out[s] = jnp.where(s < count[0], blk, jnp.zeros_like(blk))


def slots(me, row, col, count, need, parts):
    return pl.pallas_call(
        slots_kernel,
        out_shape=sds((SLOTS, 16, B), F32),
        in_specs=[SMEM] * 5 + [VMEM] * len(parts),
        out_specs=VMEM,
        scratch_shapes=[pltpu.VMEM((NZ, 4, RB * 16, 2 * B), F32)],
        compiler_params=PARAMS,
        cost_estimate=cost(0, 5 << 20),
        name="slots",
    )(me, row, col, count, need, *parts)


def shift_z(k):
    return [(y * NZ + z, y * NZ + (z + k) % NZ) for y in range(NY) for z in range(NZ)]


def shift_y(k):
    return [(y * NZ + z, (y + k) % NY * NZ + z) for y in range(NY) for z in range(NZ)]


def shift_x(k):
    return [(x * 2 + c, (x + k) % NX * 2 + c) for x in range(NX) for c in range(2)]


def tie(*trees):
    return lax.optimization_barrier(trees)


def after(a, first):
    return lax.optimization_barrier((a, first))[0]


def tie(*trees):
    return lax.optimization_barrier(trees)


def on_device(x_in, grad_pre, weight_blocks, slot_row, slot_col, slot_count):
    me = lax.axis_index("mp").astype(I32).reshape(1)
    d = lax.axis_index("dp").astype(I32).reshape(1)

    def z_step(a, k):
        return lax.ppermute(a, "mp", shift_z(k))

    def core_step(a):
        return lax.ppermute(a, "dp", [(a, a ^ 1) for a in range(2 * NX)])

    def y_back(parts):
        return [lax.ppermute(a, "mp", shift_y(k)) for a, k in zip(parts, OWNERS)]

    def x_step(out):
        return [lax.ppermute(a, "dp", shift_x(k)) for a, k in zip(out, (1, 2, 3))]

    held = {0: grad_pre}
    z1 = [z_step(grad_pre, 1), z_step(grad_pre, -1)]
    need, xt = turn(slot_col, slot_count, x_in)
    xts = [lax.ppermute(xt, "mp", shift_y(-k)) for k in OWNERS]
    own, *bufs = pack(me, d, slot_row, slot_col, slot_count, need, weight_blocks)
    z1, xts, bufs = tie(z1, xts, bufs)

    held[-1], held[1] = z1
    z2 = [z_step(z1[0], 1), z_step(z1[1], -1)]
    bufs = [lax.ppermute(a, "mp", shift_y(-k)) for a, k in zip(bufs, OWNERS)]
    xts = [xt, *xts]
    cols = heads(xts)
    z2, cols = tie(z2, cols)

    held[-2], held[2] = z2
    z3 = [z_step(z2[0], 1), z_step(z2[1], -1)]
    grads = early(me, cols, xts, [held[k] for k in EARLY])
    z3, bufs, grads = tie(z3, bufs, grads)
    early_sum = lax.psum_scatter(grads, "dp", scatter_dimension=0, tiled=True)

    held[-3], held[3] = z3
    half = T // 2
    z4 = [z_step(z3[0][:half], 1), z_step(z3[1][half:], -1)]
    near = jnp.stack(bufs)
    far = core_step(near)
    *accs, kept = inputs(me, d, cols, own, near, far, [held[k] for k in ROUNDS[0]])
    z4, accs, kept = tie(z4, accs, kept)

    total, up, down, lo, hi = rest(me, cols, kept, z4, accs)
    lo, hi = lax.ppermute(lo, "mp", shift_y(1)), lax.ppermute(hi, "mp", shift_y(-1))
    mine, other = late(me, d, cols, xts, after([held[3], held[-3], *z4], total))
    theirs = core_step(other)
    keep, *out = pair(mine, theirs)
    out = [a.astype(jnp.float16) for a in out]
    got = x_step(out)
    up, down = relay(*after((up, down), out), lo, hi)
    up, down = lax.ppermute(up, "mp", shift_y(1)), lax.ppermute(down, "mp", shift_y(-1))
    first, *back = join(early_sum, keep, [a.astype(F32) for a in got])
    parts = [first] + [a.astype(F32) for a in y_back([a.astype(jnp.float16) for a in back])]
    grad_x = (total + (up + down)).astype(BF16)
    return grad_x, slots(me, slot_row, slot_col, slot_count, after(need, grad_x), parts)


def solution(mesh):
    placed = (P("dp", "mp"), P("dp", "mp"), P("mp", None, None), P("mp"), P("mp"), P("mp"))
    return jax.shard_map(
        on_device,
        mesh=mesh,
        in_specs=placed,
        out_specs=(P("dp", "mp"), P("mp", "dp", None)),
        check_vma=False,
    )
```
